512 devices in a mesh: row: 32 (over x, y, core), col: 16 (over z).
Axes of the slice: x: 4, y: 4, z: 16, core: 2. Of those that a mesh axis runs over, the one named last changes fastest.
Arguments:
- diag_factor: float32 [1024, 1024], P('row', 'col'), may hold values from -1 to 2.5, as said below
- panel_factor: float32 [16384, 1024], P('row', 'col'), may hold values from -0.046875 to 0.046875
- left_factor: float32 [16384, 8192], P('row', 'col'), may hold values from -0.046875 to 0.046875
- pivot_factor: float32 [1024, 8192], P('row', 'col'), may hold values from -0.1875 to 0.1875
- panel_adjoint: float32 [16384, 1024], P('row', 'col'), may hold values from -6 to 6
- left_adjoint: float32 [16384, 8192], P('row', 'col'), may hold values from -6 to 6
- pivot_adjoint: float32 [1024, 8192], P('row', 'col'), may hold values from -6 to 6
- diag_adjoint: float32 [1024, 1024], P('row', 'col'), may hold values from -6 to 6
Outputs:
- solved_panel: float32 [16384, 1024], P('row', 'col')
- left_out: float32 [16384, 8192], P('row', 'col')
- pivot_out: float32 [1024, 8192], P('row', 'col')
- diag_out: float32 [1024, 1024], P('row', 'col')
The draws below stay inside these ranges and needn't reach their ends.
Inputs may be any that keep to these rules, and one draw needn't show every extreme that they name: diag_factor is lower triangular: zero above the diagonal, diagonal entries at least 1.
All inputs are finite; a program needn't handle non-finite values.
Results may differ from the reference program's by a relative error of at most 0.000073.
Values sent between devices are 32-bit elements; how exact they have to be, the bound alone decides.
A program may use at most 64 MiB of HBM per device.

```python
import jax
import jax.numpy as jnp
from jax import lax

NB = 1024
M = 16384
K = 8192


def draw_diag_factor(key, part):
    first_key, second_key = jax.random.split(jax.random.fold_in(key, 11))
    below = jnp.clip(jax.random.normal(first_key, (NB, NB), jnp.float32), -3.0, 3.0) * 0.5 / jnp.sqrt(NB * 1.0)
    middle = jax.random.uniform(second_key, (NB,), jnp.float32, 1.0, 2.0)
    row_index = lax.broadcasted_iota(jnp.int32, (NB, NB), 0)
    col_index = lax.broadcasted_iota(jnp.int32, (NB, NB), 1)
    lower = jnp.where(row_index > col_index, below, 0.0)
    return lower + jnp.where(row_index == col_index, middle[:, None], 0.0)


def block_levels(key, shape, shards, least, largest):
    factor_of = 1.0
    for position, parts in shards:
        heights = jax.random.uniform(jax.random.fold_in(jax.random.fold_in(key, 6), position), (parts,), jnp.float32, least / len(shards), largest / len(shards))
        factor_of = factor_of * jnp.repeat(jnp.exp(heights), shape[position] // parts).reshape((-1,) + (1,) * (len(shape) - 1 - position))
    return factor_of


def normal_values(stream_key, dims, spread, bound, cuts=(), held_as=jnp.bfloat16):
    values = spread * jax.random.normal(stream_key, dims, jnp.float32)
    if cuts:
        values = values * block_levels(stream_key, dims, cuts, -0.22, 0.18)
    return jnp.clip(values, -bound, bound).astype(held_as)


def setup_inputs(seed: int = 0) -> dict:
    key_list = jax.random.split(jax.random.key(seed), 9)
    diag_factor = draw_diag_factor(jax.random.fold_in(key_list[8], 71), 0)
    panel_factor = normal_values(key_list[1], (M, NB), M ** -0.5, 0.046875, ((0, 32), (1, 16)), jnp.float32)
    left_factor = normal_values(key_list[2], (M, K), M ** -0.5, 0.046875, ((0, 32), (1, 16)), jnp.float32)
    pivot_factor = normal_values(key_list[3], (NB, K), NB ** -0.5, 0.1875, ((0, 32), (1, 16)), jnp.float32)
    panel_adjoint = normal_values(key_list[4], (M, NB), 1.0, 6.0, ((0, 32), (1, 16)), jnp.float32)
    left_adjoint = normal_values(key_list[5], (M, K), 1.0, 6.0, ((0, 32), (1, 16)), jnp.float32)
    pivot_adjoint = normal_values(key_list[6], (NB, K), 1.0, 6.0, ((0, 32), (1, 16)), jnp.float32)
    diag_adjoint = normal_values(key_list[7], (NB, NB), 1.0, 6.0, ((0, 32), (1, 16)), jnp.float32)
    return dict(diag_factor=diag_factor, panel_factor=panel_factor, left_factor=left_factor, pivot_factor=pivot_factor, panel_adjoint=panel_adjoint, left_adjoint=left_adjoint, pivot_adjoint=pivot_adjoint, diag_adjoint=diag_adjoint)


def reference(diag_factor, panel_factor, left_factor, pivot_factor, panel_adjoint, left_adjoint, pivot_adjoint, diag_adjoint):
    highest = lax.Precision.HIGHEST
    solved_panel = jax.scipy.linalg.solve_triangular(diag_factor, panel_adjoint.T, trans='T', lower=True).T
    left_out = left_adjoint - jnp.dot(solved_panel.astype(jnp.float32), pivot_factor.astype(jnp.float32), precision=highest, preferred_element_type=jnp.float32)
    pivot_out = pivot_adjoint - jnp.dot(solved_panel.T.astype(jnp.float32), left_factor.astype(jnp.float32), precision=highest, preferred_element_type=jnp.float32)
    square = jnp.dot(solved_panel.T.astype(jnp.float32), panel_factor.astype(jnp.float32), precision=highest, preferred_element_type=jnp.float32)
    diag_out = diag_adjoint - jnp.tril(square)
    return (solved_panel, left_out, pivot_out, diag_out)
```

```python
import functools

import jax
import jax.numpy as jnp
from jax import lax
from jax.experimental import pallas as pl
from jax.experimental.pallas import tpu as pltpu
from jax.sharding import PartitionSpec as P

MESH = pl.DeviceIdType.MESH
F32 = jnp.float32
BF16 = jnp.bfloat16
NZ = 16
PIECES = 4


def dg(a, b, ca, cb):
    return lax.dot_general(a, b, (((ca,), (cb,)), ((), ())), preferred_element_type=F32)


def split(value):
    high = value.astype(BF16)
    return high, (value - high.astype(F32)).astype(BF16)


def mm3(a, b, ca=1, cb=0):
    return dg(a[0], b[0], ca, cb) + dg(a[0], b[1], ca, cb) + dg(a[1], b[0], ca, cb)


def invert_small(blocks, n):
    i = lax.broadcasted_iota(jnp.int32, (n, n), 0)
    j = lax.broadcasted_iota(jnp.int32, (n, n), 1)
    eye = i == j
    inverses = []
    for block in blocks:
        diagonal = jnp.where(eye, block, 0.0)
        by_row = 1.0 / jnp.sum(diagonal, axis=1, keepdims=True)
        by_col = 1.0 / jnp.sum(diagonal, axis=0, keepdims=True)
        pair = ((i // 2) == (j // 2)) & (i > j)
        inverses.append(jnp.where(eye, by_row, 0.0) - jnp.where(pair, block * by_row * by_col, 0.0))
    width = 2
    while width < n:
        mask = ((i // (2 * width)) == (j // (2 * width))) & ((i // width) > (j // width))
        parts = [split(w) for w in inverses]
        inner = [mm3(split(jnp.where(mask, d, 0.0)), w) for d, w in zip(blocks, parts)]
        inverses = [w - mm3(p, split(t)) for w, p, t in zip(inverses, parts, inner)]
        width *= 2
        yield None
    yield inverses


def kernel(
    d_ref, r_ref, at_ref, b_ref, ct_ref,
    xr_ref, xs_ref, ps_ref, ds_ref,
    abuf, dslot, dbuf, rbuf, bbuf, cbuf,
    wh, wl, ah, al, xt, xh, xl, bh, bl, rh, rl,
    own1, sib1, got1, own2, sib2, got2, far1, far2, sum1, sum2, end1, end2,
    lsem, a_s, a_r, dz_s, dz_r, d1_s, d1_r, d2_s, d2_r, d3_s, d3_r,
    r1_s, r1_r, r2_s, r2_r, r3_s, r3_r, c_s, c_r, p1_s, p1_r, p2_s, p2_r,
):
    row = lax.axis_index("row")
    z = lax.axis_index("col")
    c = lax.rem(row, 2)
    y = lax.rem(row // 2, 4)
    x = row // 8

    def x_peer(k):
        return {"row": (lax.rem(x + k, 4) * 4 + y) * 2 + c}

    def y_peer(k):
        return {"row": (x * 4 + lax.rem(y + k, 4)) * 2 + c}

    sibling = {"row": row + 1 - 2 * c}
    z_right = {"col": lax.rem(z + 1, NZ)}
    z_left = {"col": lax.rem(z + NZ - 1, NZ)}

    def remote(src, dst, send, recv, device):
        return pltpu.make_async_remote_copy(
            src_ref=src, dst_ref=dst, send_sem=send, recv_sem=recv, device_id=device, device_id_type=MESH
        )

    local_b = pltpu.make_async_copy(b_ref, bbuf, lsem.at[0])
    local_c = pltpu.make_async_copy(ct_ref, cbuf, lsem.at[1])
    local_a = pltpu.make_async_copy(at_ref, abuf.at[z], lsem.at[2])
    local_r = pltpu.make_async_copy(r_ref, rbuf.at[x, y, c], lsem.at[3])
    local_a.start()
    local_r.start()
    local_b.start()
    local_c.start()

    barrier = pltpu.get_barrier_semaphore()
    greeted = [x_peer(k) for k in (1, 2, 3)] + [y_peer(k) for k in (1, 2, 3)] + [sibling, z_right, z_left]
    for device in greeted:
        pl.semaphore_signal(barrier, inc=1, device_id=device, device_id_type=MESH)
    own_d = d_ref[...]
    dslot[z] = jnp.concatenate([own_d[:16], own_d[16:]], axis=1)
    pl.semaphore_wait(barrier, len(greeted))

    ring_d = {}

    def d_step(s):
        if s > 1:
            for d in range(2):
                ring_d[d, s - 1].wait_recv()
        if s > 8:
            return
        for d in range(2):
            if s == 8 and d == 1:
                continue
            block = lax.rem(z + NZ - (s - 1), NZ) if d == 0 else lax.rem(z + (s - 1), NZ)
            copy = remote(
                dslot.at[block], dslot.at[block], dz_s.at[d, s - 1], dz_r.at[d, s - 1], z_right if d == 0 else z_left
            )
            copy.start()
            ring_d[d, s] = copy

    ring_a = {}
    lanes = 512 // PIECES

    def a_goes(d, s, p):
        return s < 8 or (p < PIECES // 2) == (d == 0)

    def a_piece(s, p):
        if s > 1:
            for d in range(2):
                if a_goes(d, s - 1, p):
                    ring_a[d, s - 1, p].wait_recv()
        if s > 8:
            return
        for d in range(2):
            if not a_goes(d, s, p):
                continue
            block = lax.rem(z + NZ - (s - 1), NZ) if d == 0 else lax.rem(z + (s - 1), NZ)
            cut = pl.ds(p * lanes, lanes)
            src = (at_ref if s == 1 else abuf.at[block]).at[:, cut]
            copy = remote(
                src, abuf.at[block].at[:, cut], a_s.at[d, s - 1, p], a_r.at[d, s - 1, p],
                z_right if d == 0 else z_left,
            )
            copy.start()
            ring_a[d, s, p] = copy

    def a_split(block):
        value = abuf[block]
        high, low = split(value)
        ah[block] = high
        al[block] = low

    a_queue = [(s, p) for s in range(1, 9) for p in range(PIECES)]

    def a_pump(count=PIECES):
        for _ in range(count):
            if not a_queue:
                return
            s, p = a_queue.pop(0)
            a_piece(s, p)
            if p == PIECES - 1 and s > 1:
                a_split(lax.rem(z + NZ - (s - 1), NZ))
                a_split(lax.rem(z + (s - 1), NZ))

    def r_cut(px, py, half):
        return rbuf.at[px, py, c, :, pl.ds(half * 256, 256)]

    r_copies = []
    d_step(1)
    for k in (2, 1, 3):
        for half, peer in ((0, x_peer(k)), (1, y_peer(k))):
            copy = remote(
                r_ref.at[:, pl.ds(half * 256, 256)], r_cut(x, y, half), r1_s.at[half, k - 1], r1_r.at[half, k - 1], peer
            )
            copy.start()
            r_copies.append(copy)
    a_pump()
    d_step(2)
    d_step(3)
    for copy in r_copies:
        copy.wait()
    local_r.wait()
    r_far = []
    for k in (2, 1, 3):
        half0 = rbuf.at[:, y, c, :, pl.ds(0, 256)]
        half1 = rbuf.at[x, :, c, :, pl.ds(256, 256)]
        for half, cut, peer in ((0, half0, y_peer(k)), (1, half1, x_peer(k))):
            copy = remote(cut, cut, r2_s.at[half, k - 1], r2_r.at[half, k - 1], peer)
            copy.start()
            r_far.append(copy)
    d_step(4)
    local_a.wait()
    a_split(z)
    a_pump()
    d_step(5)
    d_step(6)
    d_step(7)
    a_pump()
    d_step(8)
    ring_d[0, 8].wait_recv()

    for q in range(8):
        first = dslot[2 * q]
        second = dslot[2 * q + 1]
        dbuf[x, y, c, 0:16, q * 128:(q + 1) * 128] = jnp.concatenate([first[:, :64], second[:, :64]], axis=1)
        dbuf[x, y, c, 16:32, q * 128:(q + 1) * 128] = jnp.concatenate([first[:, 64:], second[:, 64:]], axis=1)

    def when(condition, action):
        if condition is None:
            action()
        else:
            pl.when(condition)(action)

    def at_least(value, q):
        return None if q == 0 else value >= q

    x_first = (0, 3)
    d_near = {}
    for q in range(4):
        cut = dbuf.at[x, y, c, :, pl.ds(q * 256, 256)]
        for k in (2, 1, 3):
            peer = x_peer(k) if q in x_first else y_peer(k)
            d_near[q, k] = remote(cut, cut, d1_s.at[q, k - 1], d1_r.at[q, k - 1], peer)
            when(at_least(x, q), d_near[q, k].start)
    a_pump()
    d_far = {}
    for q in range(4):
        for k in (2, 1, 3):
            if q in x_first:
                when(at_least(lax.rem(x + 4 - k, 4), q), d_near[q, k].wait_recv)
            else:
                when(at_least(x, q), d_near[q, k].wait_recv)
        for k in (2, 1, 3):
            if q in x_first:
                cut = dbuf.at[pl.ds(q, 4 - q), y, c, :, pl.ds(q * 256, 256)]
                d_far[q, k] = remote(cut, cut, d2_s.at[q, k - 1], d2_r.at[q, k - 1], y_peer(k))
                d_far[q, k].start()
            else:
                cut = dbuf.at[x, :, c, :, pl.ds(q * 256, 256)]
                d_far[q, k] = remote(cut, cut, d2_s.at[q, k - 1], d2_r.at[q, k - 1], x_peer(k))
                when(at_least(x, q), d_far[q, k].start)
    local_b.wait()
    high, low = split(bbuf[...])
    bh[...] = high
    bl[...] = low
    local_c.wait()
    c_parts = split(cbuf[...])
    a_pump()
    for copy in r_far:
        copy.wait()
    r_pair = remote(rbuf.at[:, :, c], rbuf.at[:, :, c], r3_s, r3_r, sibling)
    r_pair.start()
    d_pair = []
    for q in range(4):
        for k in (2, 1, 3):
            if q in x_first:
                d_far[q, k].wait_recv()
            else:
                when(at_least(lax.rem(x + 4 - k, 4), q), d_far[q, k].wait_recv)
        cut = dbuf.at[pl.ds(q, 4 - q), :, c, :, pl.ds(q * 256, 256)]
        copy = remote(cut, cut, d3_s.at[q], d3_r.at[q], sibling)
        copy.start()
        d_pair.append(copy)
    a_pump()
    for copy in d_pair:
        copy.wait()

    def d_block(i, j, size):
        per = size // 64
        value = dbuf[:] if False else None
        del value
        rows = []
        first = i * size
        x0, y0 = first // 256, (first % 256) // 64
        if size >= 256:
            for step in range(size // 256):
                rows.append(dbuf[x0 + step, :, :, :, j * size:(j + 1) * size].reshape(256, size))
            return rows[0] if len(rows) == 1 else jnp.concatenate(rows, axis=0)
        return dbuf[x0, y0:y0 + per, :, :, j * size:(j + 1) * size].reshape(size, size)

    def w_get(i, j, size):
        cut = (slice(i * size, (i + 1) * size), slice(j * size, (j + 1) * size))
        return wh[cut], wl[cut]

    def w_put(i, j, size, value):
        high, low = split(value)
        wh[i * size:(i + 1) * size, j * size:(j + 1) * size] = high
        wl[i * size:(i + 1) * size, j * size:(j + 1) * size] = low

    result = None
    for level, result in enumerate(invert_small([d_block(k, k, 128) for k in range(8)], 128)):
        if level % 2 == 1:
            a_pump(2)
    for k in range(8):
        w_put(k, k, 128, result[k])
        if k % 2 == 0:
            wh[k * 128:(k + 1) * 128, (k + 1) * 128:(k + 2) * 128] = jnp.zeros((128, 128), BF16)
            wl[k * 128:(k + 1) * 128, (k + 1) * 128:(k + 2) * 128] = jnp.zeros((128, 128), BF16)
    for size in (128, 256, 512):
        pairs = range(0, 1024 // size, 2)
        inner = [mm3(split(d_block(k + 1, k, size)), w_get(k, k, size)) for k in pairs]
        for k, value in zip(pairs, inner):
            w_put(k + 1, k, size, -mm3(w_get(k + 1, k + 1, size), split(value)))
            if size == 256:
                wh[k * size:(k + 1) * size, (k + 1) * size:(k + 2) * size] = jnp.zeros((size, size), BF16)
                wl[k * size:(k + 1) * size, (k + 1) * size:(k + 2) * size] = jnp.zeros((size, size), BF16)
        a_pump(2)
    while a_queue:
        a_pump(1)
    r_pair.wait()
    high, low = split(rbuf[...].reshape(1024, 512))
    rh[...] = high
    rl[...] = low
    for p in range(PIECES):
        a_piece(9, p)
    a_split(lax.rem(z + 8, NZ))

    for jb in range(4):
        k0 = jb * 256
        w_parts = (wh[k0:, k0:k0 + 256], wl[k0:, k0:k0 + 256])
        a_parts = (ah[4 * jb:].reshape(1024 - k0, 512), al[4 * jb:].reshape(1024 - k0, 512))
        value = mm3(w_parts, a_parts, 0, 0)
        high, low = split(value)
        xt[4 * jb:4 * jb + 4] = value.reshape(4, 64, 512)
        xh[4 * jb:4 * jb + 4] = high.reshape(4, 64, 512)
        xl[4 * jb:4 * jb + 4] = low.reshape(4, 64, 512)

    pair_copies = {}

    def start_task(half, k):
        if half == 0:
            first = 4 * lax.rem(x + k, 4)
            x_parts = (xh[pl.ds(first, 4)].reshape(256, 512), xl[pl.ds(first, 4)].reshape(256, 512))
        else:
            other = lax.rem(y + k, 4)
            x_parts = tuple(jnp.concatenate([ref[4 * g + other] for g in range(4)], axis=0) for ref in (xh, xl))
        cut = slice(half * 256, half * 256 + 256)
        value = mm3(x_parts, (bh[:, cut], bl[:, cut])).reshape(4, 2, 32, 256)
        own, sib, got = ((own1, sib1, got1), (own2, sib2, got2))[half]
        first_core, second_core = value[:, 0], value[:, 1]
        own[k, :, 0:32] = jnp.where(c == 0, first_core, second_core)
        sib[k, :, 0:32] = jnp.where(c == 0, second_core, first_core)
        if half == 0:
            square = mm3(x_parts, c_parts, 1, 1).reshape(4, 2, 4, 8, 64)
            packed = jnp.concatenate([square[:, :, g] for g in range(4)], axis=-1)
            own[k, :, 32:40] = jnp.where(c == 0, packed[:, 0], packed[:, 1])
            sib[k, :, 32:40] = jnp.where(c == 0, packed[:, 1], packed[:, 0])
        copy = remote(sib.at[k], got.at[k], c_s.at[half, k], c_r.at[half, k], sibling)
        copy.start()
        pair_copies[half, k] = copy

    far_copies = {}

    def finish_task(half, k):
        own, _, got = ((own1, sib1, got1), (own2, sib2, got2))[half]
        far = (far1, far2)[half]
        pair_copies[half, k].wait_recv()
        own[k] = own[k] + got[k]
        if k:
            peer = x_peer(k) if half == 0 else y_peer(k)
            copy = remote(own.at[k], far.at[k - 1], p1_s.at[half, k - 1], p1_r.at[half, k - 1], peer)
            copy.start()
            far_copies[half, k] = copy

    tasks = [(half, k) for k in (2, 1, 3, 0) for half in (0, 1)]
    for position, task in enumerate(tasks):
        start_task(*task)
        if position >= 2:
            finish_task(*tasks[position - 2])
    finish_task(*tasks[-2])
    finish_task(*tasks[-1])

    def xr_part(g):
        cut = slice(g * 256, g * 256 + 256)
        x_parts = (xh[...].reshape(1024, 512)[:, cut], xl[...].reshape(1024, 512)[:, cut])
        xr_ref[cut, :] = mm3(x_parts, (rh[...], rl[...]), 0, 0)

    xr_part(0)
    end_copies = {}
    for half in range(2):
        own, far, total = ((own1, far1, sum1), (own2, far2, sum2))[half]
        end = (end1, end2)[half]
        for k in (1, 2, 3):
            far_copies[half, k].wait_recv()
        total[...] = own[0] + far[0] + far[1] + far[2]
        for k in (2, 1, 3):
            place = lax.rem((y if half == 0 else x) + k, 4)
            peer = y_peer(k) if half == 0 else x_peer(k)
            copy = remote(total.at[place], end.at[k - 1], p2_s.at[half, k - 1], p2_r.at[half, k - 1], peer)
            copy.start()
            end_copies[half, k] = copy
    xr_part(1)
    xs_ref[...] = xt[z]
    for half in range(2):
        total = (sum1, sum2)[half]
        end = (end1, end2)[half]
        for k in (1, 2, 3):
            end_copies[half, k].wait_recv()
        value = total[y if half == 0 else x] + end[0] + end[1] + end[2]
        ps_ref[:, half * 256:half * 256 + 256] = value[:32]
        if half == 0:
            for g in range(4):
                ds_ref[8 * g:8 * g + 8, :] = value[32:40, 64 * g:64 * g + 64]

    for copy in ring_d.values():
        copy.wait_send()
    for copy in ring_a.values():
        copy.wait_send()
    for q in range(4):
        for k in (1, 2, 3):
            when(at_least(x, q), d_near[q, k].wait_send)
            if q in x_first:
                d_far[q, k].wait_send()
            else:
                when(at_least(x, q), d_far[q, k].wait_send)
    for group in (pair_copies, far_copies, end_copies):
        for copy in group.values():
            copy.wait_send()


def fused(d, r, at, b, ct):
    dma = pltpu.SemaphoreType.DMA
    vmem = pltpu.VMEM
    any_space = pl.BlockSpec(memory_space=pl.ANY)
    in_vmem = pl.BlockSpec(memory_space=pltpu.VMEM)
    return pl.pallas_call(
        kernel,
        out_shape=(
            jax.ShapeDtypeStruct((512, 512), F32),
            jax.ShapeDtypeStruct((64, 512), F32),
            jax.ShapeDtypeStruct((32, 512), F32),
            jax.ShapeDtypeStruct((32, 64), F32),
        ),
        in_specs=[in_vmem, any_space, any_space, any_space, any_space],
        out_specs=(in_vmem,) * 4,
        scratch_shapes=[
            vmem((16, 64, 512), F32),
            vmem((16, 16, 128), F32),
            vmem((4, 4, 2, 32, 1024), F32),
            vmem((4, 4, 2, 32, 512), F32),
            vmem((512, 512), F32),
            vmem((64, 512), F32),
            vmem((1024, 1024), BF16),
            vmem((1024, 1024), BF16),
            vmem((16, 64, 512), BF16),
            vmem((16, 64, 512), BF16),
            vmem((16, 64, 512), F32),
            vmem((16, 64, 512), BF16),
            vmem((16, 64, 512), BF16),
            vmem((512, 512), BF16),
            vmem((512, 512), BF16),
            vmem((1024, 512), BF16),
            vmem((1024, 512), BF16),
            vmem((4, 4, 40, 256), F32),
            vmem((4, 4, 40, 256), F32),
            vmem((4, 4, 40, 256), F32),
            vmem((4, 4, 32, 256), F32),
            vmem((4, 4, 32, 256), F32),
            vmem((4, 4, 32, 256), F32),
            vmem((3, 4, 40, 256), F32),
            vmem((3, 4, 32, 256), F32),
            vmem((4, 40, 256), F32),
            vmem((4, 32, 256), F32),
            vmem((3, 40, 256), F32),
            vmem((3, 32, 256), F32),
            dma((4,)),
            dma((2, 8, PIECES)), dma((2, 8, PIECES)),
            dma((2, 8)), dma((2, 8)),
            dma((4, 3)), dma((4, 3)),
            dma((4, 3)), dma((4, 3)),
            dma((4,)), dma((4,)),
            dma((2, 3)), dma((2, 3)),
            dma((2, 3)), dma((2, 3)),
            dma, dma,
            dma((2, 4)), dma((2, 4)),
            dma((2, 3)), dma((2, 3)),
            dma((2, 3)), dma((2, 3)),
        ],
        compiler_params=pltpu.CompilerParams(
            collective_id=0, has_side_effects=True, vmem_limit_bytes=56 * 1024 * 1024
        ),
        cost_estimate=pl.CostEstimate(flops=6 * 10**9, bytes_accessed=8 * 2**20, transcendentals=0),
    )(d, r, at, b, ct)


def local(
    diag_factor,
    panel_factor,
    left_factor,
    pivot_factor,
    panel_adjoint,
    left_adjoint,
    pivot_adjoint,
    diag_adjoint,
):
    rows, width = diag_adjoint.shape
    xr, solved, pivot_sum, square_sum = fused(
        diag_factor, pivot_factor, panel_adjoint.T, left_factor, panel_factor.T
    )
    global_row = lax.axis_index("row") * rows + lax.broadcasted_iota(jnp.int32, (rows, width), 0)
    global_col = lax.axis_index("col") * width + lax.broadcasted_iota(jnp.int32, (rows, width), 1)
    left_out = left_adjoint - xr
    pivot_out = pivot_adjoint - pivot_sum
    diag_out = diag_adjoint - jnp.where(global_col <= global_row, square_sum, 0.0)
    return (solved.T, left_out, pivot_out, diag_out)


def solution(mesh):
    spec = P("row", "col")
    return jax.shard_map(
        local, mesh=mesh, in_specs=(spec,) * 8, out_specs=(spec,) * 4, check_vma=False
    )
```

```python
import functools

import jax
import jax.numpy as jnp
from jax import lax
from jax.experimental import pallas as pl
from jax.experimental.pallas import tpu as pltpu
from jax.sharding import PartitionSpec as P

MESH = pl.DeviceIdType.MESH
F32 = jnp.float32
BF16 = jnp.bfloat16
NZ = 16
PIECES = 4


def dg(a, b, ca, cb):
    return lax.dot_general(a, b, (((ca,), (cb,)), ((), ())), preferred_element_type=F32)


def split(value):
    high = value.astype(BF16)
    return high, (value - high.astype(F32)).astype(BF16)


def mm3(a, b, ca=1, cb=0):
    return dg(a[0], b[0], ca, cb) + dg(a[0], b[1], ca, cb) + dg(a[1], b[0], ca, cb)


def invert_small(blocks, n):
    i = lax.broadcasted_iota(jnp.int32, (n, n), 0)
    j = lax.broadcasted_iota(jnp.int32, (n, n), 1)
    eye = i == j
    inverses = []
    for block in blocks:
        diagonal = jnp.where(eye, block, 0.0)
        by_row = 1.0 / jnp.sum(diagonal, axis=1, keepdims=True)
        by_col = 1.0 / jnp.sum(diagonal, axis=0, keepdims=True)
        pair = ((i // 2) == (j // 2)) & (i > j)
        inverses.append(jnp.where(eye, by_row, 0.0) - jnp.where(pair, block * by_row * by_col, 0.0))
    width = 2
    while width < n:
        mask = ((i // (2 * width)) == (j // (2 * width))) & ((i // width) > (j // width))
        parts = [split(w) for w in inverses]
        inner = [mm3(split(jnp.where(mask, d, 0.0)), w) for d, w in zip(blocks, parts)]
        inverses = [w - mm3(p, split(t)) for w, p, t in zip(inverses, parts, inner)]
        width *= 2
        yield None
    yield inverses


def kernel(
    d_ref, r_ref, at_ref, b_ref, ct_ref,
    xr_ref, xs_ref, ps_ref, ds_ref,
    abuf, dslot, dbuf, rbuf, bbuf, cbuf,
    wh, wl, ah, al, xt, xh, xl, bh, bl, rh, rl,
    xrbuf, own1, sib1, got1, own2, sib2, got2, far1, far2, sum1, sum2, end1, end2,
    lsem, a_s, a_r, dz_s, dz_r, d1_s, d1_r, d2_s, d2_r, d3_s, d3_r,
    r1_s, r1_r, r2_s, r2_r, r3_s, r3_r, c_s, c_r, p1_s, p1_r, p2_s, p2_r,
):
    row = lax.axis_index("row")
    z = lax.axis_index("col")
    c = lax.rem(row, 2)
    y = lax.rem(row // 2, 4)
    x = row // 8

    def x_peer(k):
        return {"row": (lax.rem(x + k, 4) * 4 + y) * 2 + c}

    def y_peer(k):
        return {"row": (x * 4 + lax.rem(y + k, 4)) * 2 + c}

    sibling = {"row": row + 1 - 2 * c}

    def z_peer(k):
        return {"col": lax.rem(z + k + NZ, NZ)}

    z_right, z_left = z_peer(1), z_peer(-1)

    def remote(src, dst, send, recv, device):
        return pltpu.make_async_remote_copy(
            src_ref=src, dst_ref=dst, send_sem=send, recv_sem=recv, device_id=device, device_id_type=MESH
        )

    local_b = pltpu.make_async_copy(b_ref, bbuf, lsem.at[0])
    local_c = pltpu.make_async_copy(ct_ref, cbuf, lsem.at[1])
    local_a = pltpu.make_async_copy(at_ref, abuf.at[z], lsem.at[2])
    local_r = pltpu.make_async_copy(r_ref, rbuf.at[x, y, c], lsem.at[3])
    local_a.start()
    local_r.start()
    local_b.start()
    local_c.start()

    barrier = pltpu.get_barrier_semaphore()
    greeted = [x_peer(k) for k in (1, 2, 3)] + [y_peer(k) for k in (1, 2, 3)] + [sibling]
    greeted += [z_peer(k) for k in (8, 4, -4, 2, -2, 1, -1)]
    for device in greeted:
        pl.semaphore_signal(barrier, inc=1, device_id=device, device_id_type=MESH)
    own_d = d_ref[...]
    dslot[lax.rem(z, 4), z // 4] = jnp.concatenate([own_d[:16], own_d[16:]], axis=1)
    pl.semaphore_wait(barrier, len(greeted))

    d_z = {}

    def d_fours():
        cut = dslot.at[lax.rem(z, 4), z // 4]
        for i, k in enumerate((8, 4, -4)):
            d_z[i] = remote(cut, cut, dz_s.at[i], dz_r.at[i], z_peer(k))
            d_z[i].start()

    def d_near_z():
        for i in range(3):
            d_z[i].wait_recv()
        cut = dslot.at[lax.rem(z, 4)]
        for i, k in ((3, 2), (4, 1), (5, -1)):
            d_z[i] = remote(cut, cut, dz_s.at[i], dz_r.at[i], z_peer(k))
            d_z[i].start()

    ring_a = {}
    lanes = 512 // PIECES

    def a_goes(d, s, p):
        return s < 8 or (p < PIECES // 2) == (d == 0)

    def a_piece(s, p):
        if s > 1:
            for d in range(2):
                if a_goes(d, s - 1, p):
                    ring_a[d, s - 1, p].wait_recv()
        if s > 8:
            return
        for d in range(2):
            if not a_goes(d, s, p):
                continue
            block = lax.rem(z + NZ - (s - 1), NZ) if d == 0 else lax.rem(z + (s - 1), NZ)
            cut = pl.ds(p * lanes, lanes)
            src = (at_ref if s == 1 else abuf.at[block]).at[:, cut]
            copy = remote(
                src, abuf.at[block].at[:, cut], a_s.at[d, s - 1, p], a_r.at[d, s - 1, p],
                z_right if d == 0 else z_left,
            )
            copy.start()
            ring_a[d, s, p] = copy

    def a_split(block):
        value = abuf[block]
        high, low = split(value)
        ah[block] = high
        al[block] = low

    a_queue = [(s, p) for s in range(1, 9) for p in range(PIECES)]

    def a_pump(count=PIECES):
        for _ in range(count):
            if not a_queue:
                return
            s, p = a_queue.pop(0)
            a_piece(s, p)
            if p == PIECES - 1 and s > 1:
                a_split(lax.rem(z + NZ - (s - 1), NZ))
                a_split(lax.rem(z + (s - 1), NZ))

    def r_cut(px, py, half):
        return rbuf.at[px, py, c, :, pl.ds(half * 256, 256)]

    r_copies = []
    d_fours()
    for k in (2, 1, 3):
        for half, peer in ((0, x_peer(k)), (1, y_peer(k))):
            copy = remote(
                r_ref.at[:, pl.ds(half * 256, 256)], r_cut(x, y, half), r1_s.at[half, k - 1], r1_r.at[half, k - 1], peer
            )
            copy.start()
            r_copies.append(copy)
    a_pump()
    for copy in r_copies:
        copy.wait()
    local_r.wait()
    r_far = []
    for k in (2, 1, 3):
        half0 = rbuf.at[:, y, c, :, pl.ds(0, 256)]
        half1 = rbuf.at[x, :, c, :, pl.ds(256, 256)]
        for half, cut, peer in ((0, half0, y_peer(k)), (1, half1, x_peer(k))):
            copy = remote(cut, cut, r2_s.at[half, k - 1], r2_r.at[half, k - 1], peer)
            copy.start()
            r_far.append(copy)
    a_pump()
    d_near_z()
    a_pump()
    for i in (3, 4, 5):
        d_z[i].wait_recv()

    for q in range(8):
        first = dslot[(2 * q) % 4, q // 2]
        second = dslot[(2 * q + 1) % 4, q // 2]
        dbuf[x, y, c, 0:16, q * 128:(q + 1) * 128] = jnp.concatenate([first[:, :64], second[:, :64]], axis=1)
        dbuf[x, y, c, 16:32, q * 128:(q + 1) * 128] = jnp.concatenate([first[:, 64:], second[:, 64:]], axis=1)

    def when(condition, action):
        if condition is None:
            action()
        else:
            pl.when(condition)(action)

    def at_least(value, q):
        return None if q == 0 else value >= q

    x_first = (0, 2, 3)
    d_near = {}
    for q in range(4):
        cut = dbuf.at[x, y, c, :, pl.ds(q * 256, 256)]
        for k in (2, 1, 3):
            peer = x_peer(k) if q in x_first else y_peer(k)
            d_near[q, k] = remote(cut, cut, d1_s.at[q, k - 1], d1_r.at[q, k - 1], peer)
            when(at_least(x, q), d_near[q, k].start)
    a_pump()
    d_far = {}
    for q in range(4):
        for k in (2, 1, 3):
            if q in x_first:
                when(at_least(lax.rem(x + 4 - k, 4), q), d_near[q, k].wait_recv)
            else:
                when(at_least(x, q), d_near[q, k].wait_recv)
        for k in (2, 1, 3):
            if q in x_first:
                cut = dbuf.at[pl.ds(q, 4 - q), y, c, :, pl.ds(q * 256, 256)]
                d_far[q, k] = remote(cut, cut, d2_s.at[q, k - 1], d2_r.at[q, k - 1], y_peer(k))
                d_far[q, k].start()
            else:
                cut = dbuf.at[x, :, c, :, pl.ds(q * 256, 256)]
                d_far[q, k] = remote(cut, cut, d2_s.at[q, k - 1], d2_r.at[q, k - 1], x_peer(k))
                when(at_least(x, q), d_far[q, k].start)
    a_pump()
    local_a.wait()
    a_split(z)
    local_b.wait()
    high, low = split(bbuf[...])
    bh[...] = high
    bl[...] = low
    local_c.wait()
    c_parts = split(cbuf[...])
    a_pump()
    d_pair = []
    for q in range(4):
        for k in (2, 1, 3):
            if q in x_first:
                d_far[q, k].wait_recv()
            else:
                when(at_least(lax.rem(x + 4 - k, 4), q), d_far[q, k].wait_recv)
        cut = dbuf.at[pl.ds(q, 4 - q), :, c, :, pl.ds(q * 256, 256)]
        copy = remote(cut, cut, d3_s.at[q], d3_r.at[q], sibling)
        copy.start()
        d_pair.append(copy)
    a_pump()
    for copy in d_pair:
        copy.wait()

    def d_block(i, j, size):
        per = size // 64
        rows = []
        first = i * size
        x0, y0 = first // 256, (first % 256) // 64
        if size >= 256:
            for step in range(size // 256):
                rows.append(dbuf[x0 + step, :, :, :, j * size:(j + 1) * size].reshape(256, size))
            return rows[0] if len(rows) == 1 else jnp.concatenate(rows, axis=0)
        return dbuf[x0, y0:y0 + per, :, :, j * size:(j + 1) * size].reshape(size, size)

    def w_get(i, j, size):
        cut = (slice(i * size, (i + 1) * size), slice(j * size, (j + 1) * size))
        return wh[cut], wl[cut]

    def w_put(i, j, size, value):
        high, low = split(value)
        wh[i * size:(i + 1) * size, j * size:(j + 1) * size] = high
        wl[i * size:(i + 1) * size, j * size:(j + 1) * size] = low

    result = None
    for level, result in enumerate(invert_small([d_block(k, k, 128) for k in range(8)], 128)):
        if level % 2 == 1:
            a_pump(2)
    for k in range(8):
        w_put(k, k, 128, result[k])
        if k % 2 == 0:
            wh[k * 128:(k + 1) * 128, (k + 1) * 128:(k + 2) * 128] = jnp.zeros((128, 128), BF16)
            wl[k * 128:(k + 1) * 128, (k + 1) * 128:(k + 2) * 128] = jnp.zeros((128, 128), BF16)
    for size in (128, 256, 512):
        pairs = range(0, 1024 // size, 2)
        inner = [mm3(split(d_block(k + 1, k, size)), w_get(k, k, size)) for k in pairs]
        for k, value in zip(pairs, inner):
            w_put(k + 1, k, size, -mm3(w_get(k + 1, k + 1, size), split(value)))
            if size == 256:
                wh[k * size:(k + 1) * size, (k + 1) * size:(k + 2) * size] = jnp.zeros((size, size), BF16)
                wl[k * size:(k + 1) * size, (k + 1) * size:(k + 2) * size] = jnp.zeros((size, size), BF16)
        a_pump(2)
    while a_queue:
        a_pump(1)
    for copy in r_far:
        copy.wait()
    r_pair = remote(rbuf.at[:, :, c], rbuf.at[:, :, c], r3_s, r3_r, sibling)
    r_pair.start()
    for p in range(PIECES):
        a_piece(9, p)
    a_split(lax.rem(z + 8, NZ))

    for jb in range(4):
        k0 = jb * 256
        w_parts = (wh[k0:, k0:k0 + 256], wl[k0:, k0:k0 + 256])
        a_parts = (ah[4 * jb:].reshape(1024 - k0, 512), al[4 * jb:].reshape(1024 - k0, 512))
        value = mm3(w_parts, a_parts, 0, 0)
        high, low = split(value)
        xt[4 * jb:4 * jb + 4] = value.reshape(4, 64, 512)
        xh[4 * jb:4 * jb + 4] = high.reshape(4, 64, 512)
        xl[4 * jb:4 * jb + 4] = low.reshape(4, 64, 512)

    pair_copies = {}

    def start_task(half, k):
        if half == 0:
            first = 4 * lax.rem(x + k, 4)
            x_parts = (xh[pl.ds(first, 4)].reshape(256, 512), xl[pl.ds(first, 4)].reshape(256, 512))
        else:
            other = lax.rem(y + k, 4)
            x_parts = tuple(jnp.concatenate([ref[4 * g + other] for g in range(4)], axis=0) for ref in (xh, xl))
        cut = slice(half * 256, half * 256 + 256)
        value = mm3(x_parts, (bh[:, cut], bl[:, cut])).reshape(4, 2, 32, 256)
        own, sib, got = ((own1, sib1, got1), (own2, sib2, got2))[half]
        first_core, second_core = value[:, 0], value[:, 1]
        own[k, :, 0:32] = jnp.where(c == 0, first_core, second_core)
        sib[k, :, 0:32] = jnp.where(c == 0, second_core, first_core)
        if half == 0:
            square = mm3(x_parts, c_parts, 1, 1).reshape(4, 2, 4, 8, 64)
            packed = jnp.concatenate([square[:, :, g] for g in range(4)], axis=-1)
            own[k, :, 32:40] = jnp.where(c == 0, packed[:, 0], packed[:, 1])
            sib[k, :, 32:40] = jnp.where(c == 0, packed[:, 1], packed[:, 0])
        copy = remote(sib.at[k], got.at[k], c_s.at[half, k], c_r.at[half, k], sibling)
        copy.start()
        pair_copies[half, k] = copy

    far_copies = {}

    def finish_task(half, k):
        own, _, got = ((own1, sib1, got1), (own2, sib2, got2))[half]
        far = (far1, far2)[half]
        pair_copies[half, k].wait_recv()
        own[k] = own[k] + got[k]
        if k:
            peer = x_peer(k) if half == 0 else y_peer(k)
            for m in (2, 1, 3, 0):
                place = lax.rem((y if half == 0 else x) + m, 4)
                copy = remote(
                    own.at[k, place], far.at[k - 1, place], p1_s.at[half, k - 1, m], p1_r.at[half, k - 1, m], peer
                )
                copy.start()
                far_copies[half, k, m] = copy

    tasks = [(half, k) for k in (2, 1, 3, 0) for half in (0, 1)]
    for position, task in enumerate(tasks):
        start_task(*task)
        if position >= 2:
            finish_task(*tasks[position - 2])
    finish_task(*tasks[-2])
    finish_task(*tasks[-1])

    def xr_part(g):
        cut = slice(g * 256, g * 256 + 256)
        x_parts = (xh[...].reshape(1024, 512)[:, cut], xl[...].reshape(1024, 512)[:, cut])
        xrbuf[cut, :] = mm3(x_parts, (rh[...], rl[...]), 0, 0)
        copy = pltpu.make_async_copy(xrbuf.at[pl.ds(g * 256, 256)], xr_ref.at[pl.ds(g * 256, 256)], lsem.at[4 + g])
        copy.start()
        out_copies.append(copy)

    out_copies = [pltpu.make_async_copy(xt.at[z], xs_ref, lsem.at[6])]
    out_copies[0].start()

    r_pair.wait()
    high, low = split(rbuf[...].reshape(1024, 512))
    rh[...] = high
    rl[...] = low
    xr_part(0)
    xr_part(1)
    end_copies = {}
    for m in (2, 1, 3, 0):
        for half in range(2):
            own, far, total = ((own1, far1, sum1), (own2, far2, sum2))[half]
            end = (end1, end2)[half]
            place = lax.rem((y if half == 0 else x) + m, 4)
            for k in (1, 2, 3):
                far_copies[half, k, m].wait_recv()
            total[place] = own[0, place] + far[0, place] + far[1, place] + far[2, place]
            if m:
                peer = y_peer(m) if half == 0 else x_peer(m)
                copy = remote(total.at[place], end.at[m - 1], p2_s.at[half, m - 1], p2_r.at[half, m - 1], peer)
                copy.start()
                end_copies[half, m] = copy
    for half in range(2):
        total = (sum1, sum2)[half]
        end = (end1, end2)[half]
        for k in (1, 2, 3):
            end_copies[half, k].wait_recv()
        value = total[y if half == 0 else x] + end[0] + end[1] + end[2]
        ps_ref[:, half * 256:half * 256 + 256] = value[:32]
        if half == 0:
            for g in range(4):
                at_row = row * 32 + 8 * g + lax.broadcasted_iota(jnp.int32, (8, 64), 0)
                at_col = z * 64 + lax.broadcasted_iota(jnp.int32, (8, 64), 1)
                part = value[32:40, 64 * g:64 * g + 64]
                ds_ref[8 * g:8 * g + 8, :] = jnp.where(at_col <= at_row, part, 0.0)

    for copy in out_copies:
        copy.wait()
    for copy in d_z.values():
        copy.wait_send()
    for copy in ring_a.values():
        copy.wait_send()
    for q in range(4):
        for k in (1, 2, 3):
            when(at_least(x, q), d_near[q, k].wait_send)
            if q in x_first:
                d_far[q, k].wait_send()
            else:
                when(at_least(x, q), d_far[q, k].wait_send)
    for group in (pair_copies, far_copies, end_copies):
        for copy in group.values():
            copy.wait_send()


def fused(d, r, at, b, ct):
    dma = pltpu.SemaphoreType.DMA
    vmem = pltpu.VMEM
    any_space = pl.BlockSpec(memory_space=pl.ANY)
    in_vmem = pl.BlockSpec(memory_space=pltpu.VMEM)
    return pl.pallas_call(
        kernel,
        out_shape=(
            jax.ShapeDtypeStruct((512, 512), F32),
            jax.ShapeDtypeStruct((64, 512), F32),
            jax.ShapeDtypeStruct((32, 512), F32),
            jax.ShapeDtypeStruct((32, 64), F32),
        ),
        in_specs=[in_vmem, any_space, any_space, any_space, any_space],
        out_specs=(any_space, any_space, in_vmem, in_vmem),
        scratch_shapes=[
            vmem((16, 64, 512), F32),
            vmem((4, 4, 16, 128), F32),
            vmem((4, 4, 2, 32, 1024), F32),
            vmem((4, 4, 2, 32, 512), F32),
            vmem((512, 512), F32),
            vmem((64, 512), F32),
            vmem((1024, 1024), BF16),
            vmem((1024, 1024), BF16),
            vmem((16, 64, 512), BF16),
            vmem((16, 64, 512), BF16),
            vmem((16, 64, 512), F32),
            vmem((16, 64, 512), BF16),
            vmem((16, 64, 512), BF16),
            vmem((512, 512), BF16),
            vmem((512, 512), BF16),
            vmem((1024, 512), BF16),
            vmem((1024, 512), BF16),
            vmem((512, 512), F32),
            vmem((4, 4, 40, 256), F32),
            vmem((4, 4, 40, 256), F32),
            vmem((4, 4, 40, 256), F32),
            vmem((4, 4, 32, 256), F32),
            vmem((4, 4, 32, 256), F32),
            vmem((4, 4, 32, 256), F32),
            vmem((3, 4, 40, 256), F32),
            vmem((3, 4, 32, 256), F32),
            vmem((4, 40, 256), F32),
            vmem((4, 32, 256), F32),
            vmem((3, 40, 256), F32),
            vmem((3, 32, 256), F32),
            dma((7,)),
            dma((2, 8, PIECES)), dma((2, 8, PIECES)),
            dma((6,)), dma((6,)),
            dma((4, 3)), dma((4, 3)),
            dma((4, 3)), dma((4, 3)),
            dma((4,)), dma((4,)),
            dma((2, 3)), dma((2, 3)),
            dma((2, 3)), dma((2, 3)),
            dma, dma,
            dma((2, 4)), dma((2, 4)),
            dma((2, 3, 4)), dma((2, 3, 4)),
            dma((2, 3)), dma((2, 3)),
        ],
        compiler_params=pltpu.CompilerParams(
            collective_id=0, has_side_effects=True, vmem_limit_bytes=56 * 1024 * 1024
        ),
        cost_estimate=pl.CostEstimate(flops=6 * 10**9, bytes_accessed=8 * 2**20, transcendentals=0),
    )(d, r, at, b, ct)


def finish_kernel(
    left, pivot, diag, solved, xr, pivot_sum, square, solved_out, left_out, pivot_out, diag_out,
    xr_in, pivot_in, square_in, left_buf, sems,
):
    copies = [
        pltpu.make_async_copy(xr.at[pl.ds(0, 256)], xr_in.at[pl.ds(0, 256)], sems.at[0]),
        pltpu.make_async_copy(xr.at[pl.ds(256, 256)], xr_in.at[pl.ds(256, 256)], sems.at[1]),
        pltpu.make_async_copy(pivot_sum, pivot_in, sems.at[2]),
        pltpu.make_async_copy(square, square_in, sems.at[3]),
        pltpu.make_async_copy(solved, solved_out, sems.at[4]),
    ]
    for copy in copies:
        copy.start()
    outward = []
    for half in range(2):
        copies[half].wait()
        cut = pl.ds(half * 256, 256)
        left_buf[cut] = left[cut] - xr_in[cut]
        outward.append(pltpu.make_async_copy(left_buf.at[cut], left_out.at[cut], sems.at[5 + half]))
        outward[half].start()
    copies[2].wait()
    copies[3].wait()
    pivot_out[...] = pivot[...] - pivot_in[...]
    diag_out[...] = diag[...] - square_in[...]
    copies[4].wait()
    for copy in outward:
        copy.wait()


def finish(solved, left, xr, pivot, pivot_sum, diag, square):
    outs = tuple(jax.ShapeDtypeStruct(a.shape, F32) for a in (solved, left, pivot, diag))
    in_vmem = pl.BlockSpec(memory_space=pltpu.VMEM)
    any_space = pl.BlockSpec(memory_space=pl.ANY)
    return pl.pallas_call(
        finish_kernel,
        out_shape=outs,
        in_specs=[in_vmem] * 3 + [any_space] * 4,
        out_specs=(any_space, any_space, in_vmem, in_vmem),
        scratch_shapes=[
            pltpu.VMEM(xr.shape, F32),
            pltpu.VMEM(pivot_sum.shape, F32),
            pltpu.VMEM(square.shape, F32),
            pltpu.VMEM(left.shape, F32),
            pltpu.SemaphoreType.DMA((7,)),
        ],
        compiler_params=pltpu.CompilerParams(vmem_limit_bytes=60 * 1024 * 1024),
        cost_estimate=pl.CostEstimate(flops=300000, bytes_accessed=4 * 2**20, transcendentals=0),
    )(left, pivot, diag, solved, xr, pivot_sum, square)


def local(
    diag_factor,
    panel_factor,
    left_factor,
    pivot_factor,
    panel_adjoint,
    left_adjoint,
    pivot_adjoint,
    diag_adjoint,
):
    xr, solved, pivot_sum, square_sum = fused(
        diag_factor, pivot_factor, panel_adjoint.T, left_factor, panel_factor.T
    )
    solved, left_out, pivot_out, diag_out = finish(
        solved, left_adjoint, xr, pivot_adjoint, pivot_sum, diag_adjoint, square_sum
    )
    return (solved.T, left_out, pivot_out, diag_out)


def solution(mesh):
    spec = P("row", "col")
    return jax.shard_map(
        local, mesh=mesh, in_specs=(spec,) * 8, out_specs=(spec,) * 4, check_vma=False
    )
```

```python
import functools

import jax
import jax.numpy as jnp
from jax import lax
from jax.experimental import pallas as pl
from jax.experimental.pallas import tpu as pltpu
from jax.sharding import PartitionSpec as P

MESH = pl.DeviceIdType.MESH
F32 = jnp.float32
BF16 = jnp.bfloat16
NZ = 16
PIECES = 4


def dg(a, b, ca, cb):
    return lax.dot_general(a, b, (((ca,), (cb,)), ((), ())), preferred_element_type=F32)


def split(value):
    high = value.astype(BF16)
    return high, (value - high.astype(F32)).astype(BF16)


def mm3(a, b, ca=1, cb=0):
    return dg(a[0], b[0], ca, cb) + dg(a[0], b[1], ca, cb) + dg(a[1], b[0], ca, cb)


def invert_small(blocks, n):
    i = lax.broadcasted_iota(jnp.int32, (n, n), 0)
    j = lax.broadcasted_iota(jnp.int32, (n, n), 1)
    eye = i == j
    inverses = []
    for block in blocks:
        diagonal = jnp.where(eye, block, 0.0)
        by_row = 1.0 / jnp.sum(diagonal, axis=1, keepdims=True)
        by_col = 1.0 / jnp.sum(diagonal, axis=0, keepdims=True)
        pair = ((i // 2) == (j // 2)) & (i > j)
        inverses.append(jnp.where(eye, by_row, 0.0) - jnp.where(pair, block * by_row * by_col, 0.0))
    width = 2
    while width < n:
        mask = ((i // (2 * width)) == (j // (2 * width))) & ((i // width) > (j // width))
        parts = [split(w) for w in inverses]
        inner = [mm3(split(jnp.where(mask, d, 0.0)), w) for d, w in zip(blocks, parts)]
        inverses = [w - mm3(p, split(t)) for w, p, t in zip(inverses, parts, inner)]
        width *= 2
        yield None
    yield inverses


def kernel(
    d_ref, r_ref, at_ref, b_ref, ct_ref,
    xr_ref, xs_ref, ps_ref, ds_ref,
    abuf, dslot, dbuf, rbuf, bbuf, cbuf,
    wh, wl, ah, al, xt, xh, xl, bh, bl, rh, rl,
    xrbuf, own1, sib1, got1, own2, sib2, got2, far1, far2, sum1, sum2, end1, end2,
    lsem, a_s, a_r, dz_s, dz_r, d1_s, d1_r, d2_s, d2_r, d3_s, d3_r,
    r1_s, r1_r, r2_s, r2_r, r3_s, r3_r, c_s, c_r, p1_s, p1_r, p2_s, p2_r,
):
    row = lax.axis_index("row")
    z = lax.axis_index("col")
    c = lax.rem(row, 2)
    y = lax.rem(row // 2, 4)
    x = row // 8

    def x_peer(k):
        return {"row": (lax.rem(x + k, 4) * 4 + y) * 2 + c}

    def y_peer(k):
        return {"row": (x * 4 + lax.rem(y + k, 4)) * 2 + c}

    sibling = {"row": row + 1 - 2 * c}

    def z_peer(k):
        return {"col": lax.rem(z + k + NZ, NZ)}

    z_right, z_left = z_peer(1), z_peer(-1)

    def remote(src, dst, send, recv, device):
        return pltpu.make_async_remote_copy(
            src_ref=src, dst_ref=dst, send_sem=send, recv_sem=recv, device_id=device, device_id_type=MESH
        )

    local_b = pltpu.make_async_copy(b_ref, bbuf, lsem.at[0])
    local_c = pltpu.make_async_copy(ct_ref, cbuf, lsem.at[1])
    local_a = pltpu.make_async_copy(at_ref, abuf.at[z], lsem.at[2])
    local_r = pltpu.make_async_copy(r_ref, rbuf.at[x, y, c], lsem.at[3])
    local_a.start()
    local_r.start()
    local_b.start()
    local_c.start()

    barrier = pltpu.get_barrier_semaphore()
    greeted = [x_peer(k) for k in (1, 2, 3)] + [y_peer(k) for k in (1, 2, 3)] + [sibling]
    greeted += [z_peer(k) for k in (8, 4, -4, 2, -2, 1, -1)]
    for device in greeted:
        pl.semaphore_signal(barrier, inc=1, device_id=device, device_id_type=MESH)
    own_d = d_ref[...]
    dslot[lax.rem(z, 4), z // 4] = jnp.concatenate([own_d[:16], own_d[16:]], axis=1)
    pl.semaphore_wait(barrier, len(greeted))

    d_z = {}

    def d_fours():
        cut = dslot.at[lax.rem(z, 4), z // 4]
        for i, k in enumerate((8, 4, -4)):
            d_z[i] = remote(cut, cut, dz_s.at[i], dz_r.at[i], z_peer(k))
            d_z[i].start()

    def d_near_z():
        for i in range(3):
            d_z[i].wait_recv()
        cut = dslot.at[lax.rem(z, 4)]
        for i, k in ((3, 2), (4, 1), (5, -1)):
            d_z[i] = remote(cut, cut, dz_s.at[i], dz_r.at[i], z_peer(k))
            d_z[i].start()

    ring_a = {}
    lanes = 512 // PIECES

    def a_goes(d, s, p):
        return s < 8 or (p < PIECES // 2) == (d == 0)

    def a_piece(s, p):
        if s > 1:
            for d in range(2):
                if a_goes(d, s - 1, p):
                    ring_a[d, s - 1, p].wait_recv()
        if s > 8:
            return
        for d in range(2):
            if not a_goes(d, s, p):
                continue
            block = lax.rem(z + NZ - (s - 1), NZ) if d == 0 else lax.rem(z + (s - 1), NZ)
            cut = pl.ds(p * lanes, lanes)
            src = (at_ref if s == 1 else abuf.at[block]).at[:, cut]
            copy = remote(
                src, abuf.at[block].at[:, cut], a_s.at[d, s - 1, p], a_r.at[d, s - 1, p],
                z_right if d == 0 else z_left,
            )
            copy.start()
            ring_a[d, s, p] = copy

    def a_split(block):
        value = abuf[block]
        high, low = split(value)
        ah[block] = high
        al[block] = low

    a_queue = [(s, p) for s in range(1, 9) for p in range(PIECES)]

    def a_pump(count=PIECES):
        for _ in range(count):
            if not a_queue:
                return
            s, p = a_queue.pop(0)
            a_piece(s, p)
            if p == PIECES - 1 and s > 1:
                a_split(lax.rem(z + NZ - (s - 1), NZ))
                a_split(lax.rem(z + (s - 1), NZ))

    def r_cut(px, py, half):
        return rbuf.at[px, py, c, :, pl.ds(half * 256, 256)]

    r_copies = []
    d_fours()
    for k in (2, 1, 3):
        for half, peer in ((0, x_peer(k)), (1, y_peer(k))):
            copy = remote(
                r_ref.at[:, pl.ds(half * 256, 256)], r_cut(x, y, half), r1_s.at[half, k - 1], r1_r.at[half, k - 1], peer
            )
            copy.start()
            r_copies.append(copy)
    a_pump()
    for copy in r_copies:
        copy.wait()
    local_r.wait()
    r_far = []
    for k in (2, 1, 3):
        half0 = rbuf.at[:, y, c, :, pl.ds(0, 256)]
        half1 = rbuf.at[x, :, c, :, pl.ds(256, 256)]
        for half, cut, peer in ((0, half0, y_peer(k)), (1, half1, x_peer(k))):
            copy = remote(cut, cut, r2_s.at[half, k - 1], r2_r.at[half, k - 1], peer)
            copy.start()
            r_far.append(copy)
    a_pump()
    d_near_z()
    a_pump()
    for i in (3, 4, 5):
        d_z[i].wait_recv()

    for q in range(8):
        first = dslot[(2 * q) % 4, q // 2]
        second = dslot[(2 * q + 1) % 4, q // 2]
        dbuf[x, y, c, 0:16, q * 128:(q + 1) * 128] = jnp.concatenate([first[:, :64], second[:, :64]], axis=1)
        dbuf[x, y, c, 16:32, q * 128:(q + 1) * 128] = jnp.concatenate([first[:, 64:], second[:, 64:]], axis=1)

    def when(condition, action):
        if condition is None:
            action()
        else:
            pl.when(condition)(action)

    def at_least(value, q):
        return None if q == 0 else value >= q

    x_first = (0, 2, 3)
    d_near = {}
    for q in range(4):
        cut = dbuf.at[x, y, c, :, pl.ds(q * 256, 256)]
        for k in (2, 1, 3):
            peer = x_peer(k) if q in x_first else y_peer(k)
            d_near[q, k] = remote(cut, cut, d1_s.at[q, k - 1], d1_r.at[q, k - 1], peer)
            when(at_least(x, q), d_near[q, k].start)
    a_pump()
    d_far = {}
    for q in range(4):
        for k in (2, 1, 3):
            if q in x_first:
                when(at_least(lax.rem(x + 4 - k, 4), q), d_near[q, k].wait_recv)
            else:
                when(at_least(x, q), d_near[q, k].wait_recv)
        for k in (2, 1, 3):
            if q in x_first:
                cut = dbuf.at[pl.ds(q, 4 - q), y, c, :, pl.ds(q * 256, 256)]
                d_far[q, k] = remote(cut, cut, d2_s.at[q, k - 1], d2_r.at[q, k - 1], y_peer(k))
                d_far[q, k].start()
            else:
                cut = dbuf.at[x, :, c, :, pl.ds(q * 256, 256)]
                d_far[q, k] = remote(cut, cut, d2_s.at[q, k - 1], d2_r.at[q, k - 1], x_peer(k))
                when(at_least(x, q), d_far[q, k].start)
    a_pump()
    local_a.wait()
    a_split(z)
    local_b.wait()
    high, low = split(bbuf[...])
    bh[...] = high
    bl[...] = low
    local_c.wait()
    c_parts = split(cbuf[...])
    a_pump()
    d_pair = []
    for q in range(4):
        for k in (2, 1, 3):
            if q in x_first:
                d_far[q, k].wait_recv()
            else:
                when(at_least(lax.rem(x + 4 - k, 4), q), d_far[q, k].wait_recv)
        cut = dbuf.at[pl.ds(q, 4 - q), :, c, :, pl.ds(q * 256, 256)]
        copy = remote(cut, cut, d3_s.at[q], d3_r.at[q], sibling)
        copy.start()
        d_pair.append(copy)
    a_pump()
    for copy in d_pair:
        copy.wait()

    def d_block(i, j, size):
        per = size // 64
        rows = []
        first = i * size
        x0, y0 = first // 256, (first % 256) // 64
        if size >= 256:
            for step in range(size // 256):
                rows.append(dbuf[x0 + step, :, :, :, j * size:(j + 1) * size].reshape(256, size))
            return rows[0] if len(rows) == 1 else jnp.concatenate(rows, axis=0)
        return dbuf[x0, y0:y0 + per, :, :, j * size:(j + 1) * size].reshape(size, size)

    def w_get(i, j, size):
        cut = (slice(i * size, (i + 1) * size), slice(j * size, (j + 1) * size))
        return wh[cut], wl[cut]

    def w_put(i, j, size, value):
        high, low = split(value)
        wh[i * size:(i + 1) * size, j * size:(j + 1) * size] = high
        wl[i * size:(i + 1) * size, j * size:(j + 1) * size] = low

    result = None
    for level, result in enumerate(invert_small([d_block(k, k, 128) for k in range(8)], 128)):
        if level % 2 == 1:
            a_pump(2)
    for k in range(8):
        w_put(k, k, 128, result[k])
        if k % 2 == 0:
            wh[k * 128:(k + 1) * 128, (k + 1) * 128:(k + 2) * 128] = jnp.zeros((128, 128), BF16)
            wl[k * 128:(k + 1) * 128, (k + 1) * 128:(k + 2) * 128] = jnp.zeros((128, 128), BF16)
    for size in (128, 256, 512):
        pairs = range(0, 1024 // size, 2)
        inner = [mm3(split(d_block(k + 1, k, size)), w_get(k, k, size)) for k in pairs]
        for k, value in zip(pairs, inner):
            w_put(k + 1, k, size, -mm3(w_get(k + 1, k + 1, size), split(value)))
            if size == 256:
                wh[k * size:(k + 1) * size, (k + 1) * size:(k + 2) * size] = jnp.zeros((size, size), BF16)
                wl[k * size:(k + 1) * size, (k + 1) * size:(k + 2) * size] = jnp.zeros((size, size), BF16)
        a_pump(2)
    while a_queue:
        a_pump(1)
    for copy in r_far:
        copy.wait()
    r_pair = remote(rbuf.at[:, :, c], rbuf.at[:, :, c], r3_s, r3_r, sibling)
    r_pair.start()
    for p in range(PIECES):
        a_piece(9, p)
    a_split(lax.rem(z + 8, NZ))

    for jb in range(4):
        k0 = jb * 256
        w_parts = (wh[k0:, k0:k0 + 256], wl[k0:, k0:k0 + 256])
        a_parts = (ah[4 * jb:].reshape(1024 - k0, 512), al[4 * jb:].reshape(1024 - k0, 512))
        value = mm3(w_parts, a_parts, 0, 0)
        high, low = split(value)
        xt[4 * jb:4 * jb + 4] = value.reshape(4, 64, 512)
        xh[4 * jb:4 * jb + 4] = high.reshape(4, 64, 512)
        xl[4 * jb:4 * jb + 4] = low.reshape(4, 64, 512)

    pair_copies = {}

    def start_task(half, k):
        if half == 0:
            first = 4 * lax.rem(x + k, 4)
            x_parts = (xh[pl.ds(first, 4)].reshape(256, 512), xl[pl.ds(first, 4)].reshape(256, 512))
        else:
            other = lax.rem(y + k, 4)
            x_parts = tuple(jnp.concatenate([ref[4 * g + other] for g in range(4)], axis=0) for ref in (xh, xl))
        cut = slice(half * 256, half * 256 + 256)
        value = mm3(x_parts, (bh[:, cut], bl[:, cut])).reshape(4, 2, 32, 256)
        own, sib, got = ((own1, sib1, got1), (own2, sib2, got2))[half]
        first_core, second_core = value[:, 0], value[:, 1]
        own[k, :, 0:32] = jnp.where(c == 0, first_core, second_core)
        sib[k, :, 0:32] = jnp.where(c == 0, second_core, first_core)
        if half == 0:
            square = mm3(x_parts, c_parts, 1, 1).reshape(4, 2, 4, 8, 64)
            packed = jnp.concatenate([square[:, :, g] for g in range(4)], axis=-1)
            own[k, :, 32:40] = jnp.where(c == 0, packed[:, 0], packed[:, 1])
            sib[k, :, 32:40] = jnp.where(c == 0, packed[:, 1], packed[:, 0])
        copy = remote(sib.at[k], got.at[k], c_s.at[half, k], c_r.at[half, k], sibling)
        copy.start()
        pair_copies[half, k] = copy

    far_copies = {}

    def finish_task(half, k):
        own, _, got = ((own1, sib1, got1), (own2, sib2, got2))[half]
        far = (far1, far2)[half]
        pair_copies[half, k].wait_recv()
        own[k] = own[k] + got[k]
        if k:
            peer = x_peer(k) if half == 0 else y_peer(k)
            for m in (2, 1, 3, 0):
                place = lax.rem((y if half == 0 else x) + m, 4)
                copy = remote(
                    own.at[k, place], far.at[k - 1, place], p1_s.at[half, k - 1, m], p1_r.at[half, k - 1, m], peer
                )
                copy.start()
                far_copies[half, k, m] = copy

    tasks = [(half, k) for k in (2, 1, 3, 0) for half in (0, 1)]
    for position, task in enumerate(tasks):
        start_task(*task)
        if position >= 2:
            finish_task(*tasks[position - 2])
    finish_task(*tasks[-2])
    finish_task(*tasks[-1])

    def xr_part(g):
        cut = slice(g * 256, g * 256 + 256)
        x_parts = (xh[...].reshape(1024, 512)[:, cut], xl[...].reshape(1024, 512)[:, cut])
        xrbuf[cut, :] = mm3(x_parts, (rh[...], rl[...]), 0, 0)
        copy = pltpu.make_async_copy(xrbuf.at[pl.ds(g * 256, 256)], xr_ref.at[pl.ds(g * 256, 256)], lsem.at[4 + g])
        copy.start()
        out_copies.append(copy)

    out_copies = [pltpu.make_async_copy(xt.at[z], xs_ref, lsem.at[6])]
    out_copies[0].start()

    r_pair.wait()
    high, low = split(rbuf[...].reshape(1024, 512))
    rh[...] = high
    rl[...] = low
    xr_part(0)
    xr_part(1)
    end_copies = {}
    for m in (2, 1, 3, 0):
        for half in range(2):
            own, far, total = ((own1, far1, sum1), (own2, far2, sum2))[half]
            end = (end1, end2)[half]
            place = lax.rem((y if half == 0 else x) + m, 4)
            for k in (1, 2, 3):
                far_copies[half, k, m].wait_recv()
            total[place] = own[0, place] + far[0, place] + far[1, place] + far[2, place]
            if m:
                peer = y_peer(m) if half == 0 else x_peer(m)
                copy = remote(total.at[place], end.at[m - 1], p2_s.at[half, m - 1], p2_r.at[half, m - 1], peer)
                copy.start()
                end_copies[half, m] = copy
    for half in range(2):
        total = (sum1, sum2)[half]
        end = (end1, end2)[half]
        for k in (1, 2, 3):
            end_copies[half, k].wait_recv()
        value = total[y if half == 0 else x] + end[0] + end[1] + end[2]
        ps_ref[:, half * 256:half * 256 + 256] = value[:32]
        if half == 0:
            for g in range(4):
                at_row = row * 32 + 8 * g + lax.broadcasted_iota(jnp.int32, (8, 64), 0)
                at_col = z * 64 + lax.broadcasted_iota(jnp.int32, (8, 64), 1)
                part = value[32:40, 64 * g:64 * g + 64]
                ds_ref[8 * g:8 * g + 8, :] = jnp.where(at_col <= at_row, part, 0.0)

    for copy in out_copies:
        copy.wait()
    for copy in d_z.values():
        copy.wait_send()
    for copy in ring_a.values():
        copy.wait_send()
    for q in range(4):
        for k in (1, 2, 3):
            when(at_least(x, q), d_near[q, k].wait_send)
            if q in x_first:
                d_far[q, k].wait_send()
            else:
                when(at_least(x, q), d_far[q, k].wait_send)
    for group in (pair_copies, far_copies, end_copies):
        for copy in group.values():
            copy.wait_send()


def fused(d, r, at, b, ct):
    dma = pltpu.SemaphoreType.DMA
    vmem = pltpu.VMEM
    any_space = pl.BlockSpec(memory_space=pl.ANY)
    in_vmem = pl.BlockSpec(memory_space=pltpu.VMEM)
    return pl.pallas_call(
        kernel,
        out_shape=(
            jax.ShapeDtypeStruct((512, 512), F32),
            jax.ShapeDtypeStruct((64, 512), F32),
            jax.ShapeDtypeStruct((32, 512), F32),
            jax.ShapeDtypeStruct((32, 64), F32),
        ),
        in_specs=[in_vmem, any_space, any_space, any_space, any_space],
        out_specs=(any_space, any_space, in_vmem, in_vmem),
        scratch_shapes=[
            vmem((16, 64, 512), F32),
            vmem((4, 4, 16, 128), F32),
            vmem((4, 4, 2, 32, 1024), F32),
            vmem((4, 4, 2, 32, 512), F32),
            vmem((512, 512), F32),
            vmem((64, 512), F32),
            vmem((1024, 1024), BF16),
            vmem((1024, 1024), BF16),
            vmem((16, 64, 512), BF16),
            vmem((16, 64, 512), BF16),
            vmem((16, 64, 512), F32),
            vmem((16, 64, 512), BF16),
            vmem((16, 64, 512), BF16),
            vmem((512, 512), BF16),
            vmem((512, 512), BF16),
            vmem((1024, 512), BF16),
            vmem((1024, 512), BF16),
            vmem((512, 512), F32),
            vmem((4, 4, 40, 256), F32),
            vmem((4, 4, 40, 256), F32),
            vmem((4, 4, 40, 256), F32),
            vmem((4, 4, 32, 256), F32),
            vmem((4, 4, 32, 256), F32),
            vmem((4, 4, 32, 256), F32),
            vmem((3, 4, 40, 256), F32),
            vmem((3, 4, 32, 256), F32),
            vmem((4, 40, 256), F32),
            vmem((4, 32, 256), F32),
            vmem((3, 40, 256), F32),
            vmem((3, 32, 256), F32),
            dma((7,)),
            dma((2, 8, PIECES)), dma((2, 8, PIECES)),
            dma((6,)), dma((6,)),
            dma((4, 3)), dma((4, 3)),
            dma((4, 3)), dma((4, 3)),
            dma((4,)), dma((4,)),
            dma((2, 3)), dma((2, 3)),
            dma((2, 3)), dma((2, 3)),
            dma, dma,
            dma((2, 4)), dma((2, 4)),
            dma((2, 3, 4)), dma((2, 3, 4)),
            dma((2, 3)), dma((2, 3)),
        ],
        compiler_params=pltpu.CompilerParams(
            collective_id=0, has_side_effects=True, vmem_limit_bytes=56 * 1024 * 1024
        ),
        cost_estimate=pl.CostEstimate(flops=6 * 10**9, bytes_accessed=8 * 2**20, transcendentals=0),
    )(d, r, at, b, ct)


QUARTERS = 4


def finish_kernel(
    solved, left, xr, pivot, pivot_sum, diag, square, solved_out, left_out, pivot_out, diag_out,
    solved_buf, left_buf, xr_buf, pivot_buf, pivot_in, diag_buf, square_in, in_sems, out_sems,
):
    rows = left.shape[0] // QUARTERS
    cuts = [pl.ds(part * rows, rows) for part in range(QUARTERS)]
    pairs = []
    for cut in cuts:
        pairs += [(left.at[cut], left_buf.at[cut]), (xr.at[cut], xr_buf.at[cut])]
    pairs += [(solved, solved_buf), (pivot, pivot_buf), (pivot_sum, pivot_in), (diag, diag_buf), (square, square_in)]
    inward = [pltpu.make_async_copy(src, dst, in_sems.at[i]) for i, (src, dst) in enumerate(pairs)]
    for copy in inward:
        copy.start()
    outward = []

    def send_out(src, dst):
        copy = pltpu.make_async_copy(src, dst, out_sems.at[len(outward)])
        copy.start()
        outward.append(copy)

    for part, cut in enumerate(cuts):
        inward[2 * part].wait()
        inward[2 * part + 1].wait()
        left_buf[cut] = left_buf[cut] - xr_buf[cut]
        send_out(left_buf.at[cut], left_out.at[cut])
    small = inward[2 * QUARTERS:]
    small[0].wait()
    send_out(solved_buf, solved_out)
    small[1].wait()
    small[2].wait()
    pivot_buf[...] = pivot_buf[...] - pivot_in[...]
    send_out(pivot_buf, pivot_out)
    small[3].wait()
    small[4].wait()
    diag_buf[...] = diag_buf[...] - square_in[...]
    send_out(diag_buf, diag_out)
    for copy in outward:
        copy.wait()


def finish(*arrays):
    solved, left, _, pivot, _, diag, _ = arrays
    any_space = pl.BlockSpec(memory_space=pl.ANY)
    return pl.pallas_call(
        finish_kernel,
        out_shape=tuple(jax.ShapeDtypeStruct(a.shape, F32) for a in (solved, left, pivot, diag)),
        in_specs=[any_space] * 7,
        out_specs=(any_space,) * 4,
        scratch_shapes=[pltpu.VMEM(a.shape, F32) for a in arrays]
        + [pltpu.SemaphoreType.DMA((2 * QUARTERS + 5,)), pltpu.SemaphoreType.DMA((QUARTERS + 3,))],
        compiler_params=pltpu.CompilerParams(vmem_limit_bytes=60 * 1024 * 1024),
        cost_estimate=pl.CostEstimate(flops=300000, bytes_accessed=4 * 2**20, transcendentals=0),
    )(*arrays)


def local(
    diag_factor,
    panel_factor,
    left_factor,
    pivot_factor,
    panel_adjoint,
    left_adjoint,
    pivot_adjoint,
    diag_adjoint,
):
    xr, solved, pivot_sum, square_sum = fused(
        diag_factor, pivot_factor, panel_adjoint.T, left_factor, panel_factor.T
    )
    solved, left_out, pivot_out, diag_out = finish(
        solved, left_adjoint, xr, pivot_adjoint, pivot_sum, diag_adjoint, square_sum
    )
    return (solved.T, left_out, pivot_out, diag_out)


def solution(mesh):
    spec = P("row", "col")
    return jax.shard_map(
        local, mesh=mesh, in_specs=(spec,) * 8, out_specs=(spec,) * 4, check_vma=False
    )
```
